768 devices in a mesh: row: 32 (over y, z_lo), col: 24 (over x, z_hi, core).
Axes of the slice: x: 4, y: 8, z: 12 (z_hi: 3, z_lo: 4; z = z_hi * 4 + z_lo), core: 2. Of those that a mesh axis runs over, the one named last changes fastest.
Arguments:
- curl_tiles: bfloat16 [32, 768, 24576], P(None, 'col', 'row'), may hold values from -0.00024414062 to 0.00024414062
- gradient: bfloat16 [24576, 1536], P(('row', 'col')), may hold values from -6 to 6
- a_pattern: int32 [192, 192], replicated, may hold values 0 or 1
- g_pattern: int32 [192, 12], replicated, may hold values 0 or 1
Outputs:
- galerkin: float32 [1536, 1536], P('row', 'col')
The draws below stay inside these ranges and needn't reach their ends.
Inputs may be any that keep to these rules, and one draw needn't show every extreme that they name: `a_pattern`: 1 keeps a block in the pattern, 0 leaves it out. `g_pattern`: 1 keeps a block in the pattern, 0 leaves it out.
All inputs are finite; a program needn't handle non-finite values.
Results may differ from the reference program's by a relative error of at most 0.0003.
Values may be sent and summed in bfloat16 or wider, within the bound.
A program may use at most 32 MiB of HBM per device.

```python
import jax
import jax.numpy as jnp
from jax import lax

BLOCK = 128
CB = 12
ROW_SPAN = 768
FINE = 24576
FINE_BLOCKS = 192
COARSE = 1536
N_ROW = 32


def with_ends(result, stream_key, low, high):
    dims = result.shape
    place = [jax.random.randint(jax.random.fold_in(stream_key, axis), (), 0, dims[axis]) for axis in range(len(dims))]
    result = result.at[tuple(place)].set(low)
    longest = dims.index(max(dims))
    place[longest] = (place[longest] + 1) % dims[longest]
    return result.at[tuple(place)].set(high)


def block_levels(key, shape, split, smallest, top_value):
    gain, own = 1.0, jax.random.fold_in(key, 6)
    for dim, shards_of in split:
        heights = jnp.exp(jax.random.uniform(jax.random.fold_in(own, dim), (shards_of,), jnp.float32, smallest / len(split), top_value / len(split)))
        gain = gain * jnp.repeat(heights, shape[dim] // shards_of).reshape([-1 if axis == dim else 1 for axis in range(len(shape))])
    return gain


def noise(own_key, extent, deviation, most, cuts=(), dtype=jnp.bfloat16):
    level = block_levels(own_key, extent, cuts, -0.22, 0.18) if cuts else 1.0
    values = jax.random.normal(own_key, extent, jnp.float32) * deviation * level
    return jnp.minimum(jnp.maximum(values, -most), most).astype(dtype)


def setup_inputs(seed: int = 0) -> dict:
    seeds = jax.random.split(jax.random.key(seed), 5)
    return {
        "curl_tiles": noise(seeds[0], (N_ROW, ROW_SPAN, FINE), (FINE * FINE) ** -0.5, 0.00024414062, ((1, 24), (2, 32))),
        "gradient": noise(seeds[1], (FINE, COARSE), 1.0, 6.0, ((0, 768),)),
        "a_pattern": with_ends((jax.random.randint(seeds[2], (FINE_BLOCKS, FINE_BLOCKS), 0, 4) < 3).astype(jnp.int32), jax.random.fold_in(seeds[2], 1), 0, 1),
        "g_pattern": with_ends((jax.random.randint(seeds[3], (FINE_BLOCKS, CB), 0, 4) < 3).astype(jnp.int32), jax.random.fold_in(seeds[3], 1), 0, 1),
    }


def reference(curl_tiles, gradient, a_pattern, g_pattern):
    blocks = FINE // BLOCK
    a_full = jnp.transpose(curl_tiles.astype(jnp.float32), (2, 0, 1)).reshape(FINE, FINE)
    a_mask = a_pattern.astype(jnp.float32)[:, None, :, None]
    a_full = (a_full.reshape(blocks, BLOCK, blocks, BLOCK) * a_mask).reshape(FINE, FINE)
    g_mask = g_pattern.astype(jnp.float32)[:, None, :, None]
    g_full = (gradient.astype(jnp.float32).reshape(blocks, BLOCK, CB, BLOCK) * g_mask).reshape(FINE, COARSE)
    product = jnp.dot(a_full, g_full, precision=lax.Precision.HIGHEST, preferred_element_type=jnp.float32)
    return jnp.dot(g_full.T, product, precision=lax.Precision.HIGHEST, preferred_element_type=jnp.float32)
```

```python
import jax
import jax.numpy as jnp
from jax import lax
from jax.experimental import pallas as pl
from jax.experimental.pallas import tpu as pltpu
from jax.sharding import PartitionSpec as P

BLOCK = 128
NX, NY, NZL, NZH, NC = 4, 8, 4, 3, 2
NT = 3
F32, BF16 = jnp.float32, jnp.bfloat16

SITES = {}
TOTAL = 0


def site(name, count=1):
    global TOTAL
    SITES[name] = TOTAL
    TOTAL += count


for t in range(NT):
    site(("z", t), 4)
    for hop in range(1, 5):
        for side in "RL":
            site(("y", t, hop, side), 2)
    site(("cx", t))
    for side in "RL":
        site(("x", t, side), 3)
        site(("q", t, side), 4)
    site(("qc", t))
    site(("f", t), 4)
site("gz", 3)
for side in "RL":
    site(("gx", side), 2)
site("out")


def kernel(a_hbm, g_ref, ap_ref, gp_ref, out_ref, a_buf, at, gm, gs, gr, grt, po, pm, cx, xr, q, qcr, yr, zr, fin, fx,
           a_sem, ssem, rsem):
    row, col = lax.axis_index("row"), lax.axis_index("col")
    y, zl = row // NZL, row % NZL
    x, zh, core = col // (NZH * NC), (col // NC) % NZH, col % NC
    sib = 1 - core

    def mod(v, n):
        return lax.rem(v + n, n)

    def dev(dx=0, dy=0, dzl=0, dzh=0, other=False):
        yy, zz = mod(y + dy, NY), mod(zl + dzl, NZL)
        xx, hh = mod(x + dx, NX), mod(zh + dzh, NZH)
        cc = sib if other else core
        return (yy * NZL + zz, xx * (NZH * NC) + hh * NC + cc)

    drains = []

    def send(name, k, src, dst, to):
        i = SITES[name] + k
        copy = pltpu.make_async_remote_copy(
            src_ref=src, dst_ref=dst, send_sem=ssem.at[i], recv_sem=rsem.at[i],
            device_id=to, device_id_type=pl.DeviceIdType.MESH)
        copy.start()
        drains.append(copy)

    def arrived(name, k, dst):
        i = SITES[name] + k
        pltpu.make_async_remote_copy(
            src_ref=dst, dst_ref=dst, send_sem=ssem.at[i], recv_sem=rsem.at[i],
            device_id=dev(dy=1), device_id_type=pl.DeviceIdType.MESH).wait_recv()

    def drain(keep=0):
        while len(drains) > keep:
            drains.pop(0).wait_send()

    load_a = pltpu.make_async_copy(a_hbm, a_buf, a_sem)
    load_a.start()

    barrier = pltpu.get_barrier_semaphore()
    peers = [dev(dzl=i, dzh=h) for h in range(NZH) for i in range(NZL) if i or h]
    peers += [dev(dy=1), dev(dy=-1), dev(dx=1), dev(dx=-1), dev(other=True)]
    for peer in peers:
        pl.semaphore_signal(barrier, inc=1, device_id=peer, device_id_type=pl.DeviceIdType.MESH)

    own_block = row * 6 + col // 4
    keep = gp_ref[pl.ds(own_block, 1), :].astype(F32)
    for p in range(12):
        part = slice(p * BLOCK, (p + 1) * BLOCK)
        gm[:, part] = (g_ref[:, part].astype(F32) * jnp.broadcast_to(keep[:, p:p + 1], (32, BLOCK))).astype(BF16)
    me_m = x * NZH + zh
    gr[pl.ds(pl.multiple_of(me_m * 32, 32), 32), :] = gm[...]
    for t in range(NT):
        jj = mod(zh + 1 + t, NZH)
        for xx in range(NX):
            off = pl.multiple_of(xx * 384 + jj * BLOCK, BLOCK)
            gs[t, y, zl, :, xx * BLOCK:(xx + 1) * BLOCK] = gm[:, pl.ds(off, BLOCK)]

    pl.semaphore_wait(barrier, len(peers))

    def send_z(t):
        for i in range(1, NZL):
            send(("z", t), i, gs.at[t, y, zl], gs.at[t, y, zl], dev(dzl=i))

    def y_part(t, yy, p):
        return gs.at[t, mod(yy + NY, NY), pl.ds(2 * p, 2)]

    def a1(t):
        for i in range(1, NZL):
            arrived(("z", t), i, gs.at[t, y, mod(zl - i, NZL)])
        for p in range(2):
            ref = y_part(t, y, p)
            send(("y", t, 1, "R"), p, ref, ref, dev(dy=1))
            send(("y", t, 1, "L"), p, ref, ref, dev(dy=-1))

    def forward(t, hop):
        for p in range(2):
            ref = y_part(t, y - (hop - 1), p)
            arrived(("y", t, hop - 1, "R"), p, ref)
            if hop < 4 or p == 0:
                send(("y", t, hop, "R"), p, ref, ref, dev(dy=1))
            ref = y_part(t, y + (hop - 1), p)
            arrived(("y", t, hop - 1, "L"), p, ref)
            if hop < 4 or p == 1:
                send(("y", t, hop, "L"), p, ref, ref, dev(dy=-1))

    def a5(t):
        arrived(("y", t, 4, "R"), 0, y_part(t, y - 4, 0))
        arrived(("y", t, 4, "L"), 1, y_part(t, y + 4, 1))

    def prepare_a():
        load_a.wait()
        ap = ap_ref[...].astype(F32).astype(BF16)
        want = lax.broadcasted_iota(jnp.int32, (8, 192), 0) + row * 6
        pick = jnp.where(want == lax.broadcasted_iota(jnp.int32, (8, 192), 1), 1.0, 0.0).astype(BF16)
        rows = jnp.dot(pick, ap, preferred_element_type=F32).astype(BF16)
        want = (lax.broadcasted_iota(jnp.int32, (192, 1024), 1) // 32) * 6 + col // 4
        pick = jnp.where(want == lax.broadcasted_iota(jnp.int32, (192, 1024), 0), 1.0, 0.0).astype(BF16)
        mask = jnp.dot(rows, pick, preferred_element_type=F32)
        for b in range(6):
            block = a_buf[:, :, b * BLOCK:(b + 1) * BLOCK].reshape(1024, BLOCK)
            turned = (block.T.astype(F32) * mask[b:b + 1, :]).astype(BF16)
            for i in range(4):
                at[i % 2, (2 * b + i // 2) * 32:(2 * b + i // 2 + 1) * 32, :] = turned[i * 32:(i + 1) * 32]

    def g0():
        own = gr.at[pl.ds(pl.multiple_of(me_m * 32, 32), 32)]
        for h in range(1, NZH):
            send("gz", h, own, own, dev(dzh=h))

    def gx_rows(xx, first=0, count=96):
        return gr.at[pl.ds(pl.multiple_of(mod(xx + NX, NX) * 96 + first, 16), count)]

    def g1():
        for h in range(1, NZH):
            m = x * NZH + mod(zh - h, NZH)
            arrived("gz", h, gr.at[pl.ds(pl.multiple_of(m * 32, 32), 32)])
        send(("gx", "R"), 0, gx_rows(x), gx_rows(x), dev(dx=1))
        send(("gx", "L"), 0, gx_rows(x), gx_rows(x), dev(dx=-1))

    def g2():
        arrived(("gx", "R"), 0, gx_rows(x - 1))
        send(("gx", "R"), 1, gx_rows(x - 1, 0, 48), gx_rows(x - 1, 0, 48), dev(dx=1))
        arrived(("gx", "L"), 0, gx_rows(x + 1))
        send(("gx", "L"), 1, gx_rows(x + 1, 48, 48), gx_rows(x + 1, 48, 48), dev(dx=-1))

    def g3():
        arrived(("gx", "R"), 1, gx_rows(x - 2, 0, 48))
        arrived(("gx", "L"), 1, gx_rows(x + 2, 48, 48))
        for b in range(3):
            part = slice(b * BLOCK, (b + 1) * BLOCK)
            grt[:, part] = gr[part, :].T

    def product(t, half, out):
        for n in range(2):
            b = gs[t, :, :, :, n * 256:(n + 1) * 256].reshape(1024, 256)
            r = jnp.dot(at[half], b, preferred_element_type=F32)
            out[t, 2 * n] = r[:, :BLOCK]
            out[t, 2 * n + 1] = r[:, BLOCK:]

    def r0(t):
        product(t, sib, po)
        send(("cx", t), 0, po.at[t], cx.at[t], dev(other=True))
        product(t, core, pm)

    xp, xm, xo = mod(x + 1, NX), mod(x - 1, NX), mod(x + 2, NX)
    A, B = pl.ds(0, 192), pl.ds(192, 192)

    def r1(t):
        arrived(("cx", t), 0, cx.at[t])
        pm[t, xo] += cx[t, xo]
        send(("x", t, "R"), 0, pm.at[t, xo, A], xr.at[t, 0], dev(dx=1))
        send(("x", t, "L"), 0, pm.at[t, xo, B], xr.at[t, 3], dev(dx=-1))
        pm[t, xp] += cx[t, xp]
        send(("x", t, "R"), 1, pm.at[t, xp, B], xr.at[t, 1], dev(dx=1))
        pm[t, xm] += cx[t, xm]
        send(("x", t, "L"), 1, pm.at[t, xm, A], xr.at[t, 4], dev(dx=-1))
        pm[t, x] += cx[t, x]

    def r2(t):
        arrived(("x", t, "R"), 0, xr.at[t, 0])
        pm[t, xp, A] += xr[t, 0]
        send(("x", t, "R"), 2, pm.at[t, xp, A], xr.at[t, 2], dev(dx=1))
        arrived(("x", t, "L"), 0, xr.at[t, 3])
        pm[t, xm, B] += xr[t, 3]
        send(("x", t, "L"), 2, pm.at[t, xm, B], xr.at[t, 5], dev(dx=-1))

    def r3(t):
        for k in (1, 2):
            arrived(("x", t, "R"), k, xr.at[t, k])
            arrived(("x", t, "L"), k, xr.at[t, 3 + k])
        total = pm[t, x]
        upper = total[:192] + (xr[t, 2] + xr[t, 4])
        lower = total[192:] + (xr[t, 1] + xr[t, 5])
        total = jnp.concatenate([upper, lower], axis=0)
        high = total.astype(BF16)
        low = (total - high.astype(F32)).astype(BF16)
        r = jnp.dot(grt[...], jnp.concatenate([high, low], axis=1), preferred_element_type=F32)
        r = (r[:, :BLOCK] + r[:, BLOCK:]).reshape(32, 2, 24, BLOCK)
        q[t, 0] = r[:, 0]
        q[t, 1] = r[:, 1]
        send(("qc", t), 0, q.at[t, sib], qcr.at[t], dev(other=True))

    def q_rows(t, dy):
        return q.at[t, core, pl.ds(mod(y + dy + NY, NY) * NZL, NZL)]

    def q_half(t, dy, p):
        return q.at[t, core, pl.ds(mod(y + dy + NY, NY) * NZL + 2 * p, 2)]

    def r4(t):
        arrived(("qc", t), 0, qcr.at[t])
        q[t, core] += qcr[t]
        send(("q", t, "R"), 0, q_half(t, 4, 0), yr.at[t, 0, 0, pl.ds(0, 2)], dev(dy=1))
        send(("q", t, "L"), 0, q_half(t, -4, 1), yr.at[t, 1, 0, pl.ds(2, 2)], dev(dy=-1))

    def y_step(t, k):
        if k == 1:
            arrived(("q", t, "R"), 0, yr.at[t, 0, 0, pl.ds(0, 2)])
            q_half(t, 3, 0)[...] += yr[t, 0, 0, 0:2]
        else:
            arrived(("q", t, "R"), k - 1, yr.at[t, 0, k - 1])
            q_rows(t, 4 - k)[...] += yr[t, 0, k - 1]
        send(("q", t, "R"), k, q_rows(t, 4 - k), yr.at[t, 0, k], dev(dy=1))
        if k == 1:
            arrived(("q", t, "L"), 0, yr.at[t, 1, 0, pl.ds(2, 2)])
            q_half(t, -3, 1)[...] += yr[t, 1, 0, 2:4]
        else:
            arrived(("q", t, "L"), k - 1, yr.at[t, 1, k - 1])
            q_rows(t, k - 4)[...] += yr[t, 1, k - 1]
        send(("q", t, "L"), k, q_rows(t, k - 4), yr.at[t, 1, k], dev(dy=-1))

    def r8(t):
        arrived(("q", t, "R"), 3, yr.at[t, 0, 3])
        arrived(("q", t, "L"), 3, yr.at[t, 1, 3])
        fin[t] = q_rows(t, 0)[...] + (yr[t, 0, 3] + yr[t, 1, 3])
        for i in range(NZL):
            if t < 2 or i:
                send(("f", t), i, fin.at[t, mod(zl + i, NZL)], zr.at[t, i], dev(dzl=i, dzh=t + 1))

    def finish():
        total = fin[2, zl]
        for t in range(NT):
            for i in range(NZL):
                if t < 2 or i:
                    arrived(("f", t), i, zr.at[t, i])
                    total = total + zr[t, i]
        fx[0] = total
        send("out", 0, fx.at[0], fx.at[1], dev(other=True))
        arrived("out", 0, fx.at[1])
        theirs = fx[1]
        mine = jnp.where(core == 0, total[:, :64], total[:, 64:])
        theirs = jnp.where(core == 0, theirs[:, :64], theirs[:, 64:])
        out_ref[0:24, :] = jnp.where(core == 0, mine, theirs)
        out_ref[24:48, :] = jnp.where(core == 0, theirs, mine)

    for t in range(NT):
        send_z(t)
    g0()
    a1(0)
    prepare_a()
    forward(0, 2)
    g1()
    forward(0, 3)
    forward(0, 4)
    a1(1)
    g2()
    a5(0)
    r0(0)
    forward(1, 2)
    r1(0)
    forward(1, 3)
    r2(0)
    forward(1, 4)
    a1(2)
    g3()
    r3(0)
    a5(1)
    r0(1)
    r4(0)
    forward(2, 2)
    r1(1)
    y_step(0, 1)
    forward(2, 3)
    r2(1)
    y_step(0, 2)
    forward(2, 4)
    r3(1)
    y_step(0, 3)
    a5(2)
    r0(2)
    r8(0)
    r4(1)
    r1(2)
    y_step(1, 1)
    r2(2)
    y_step(1, 2)
    r3(2)
    y_step(1, 3)
    r4(2)
    r8(1)
    for k in (1, 2, 3):
        y_step(2, k)
    r8(2)
    finish()
    drain()


def body(curl_tiles, gradient, a_pattern, g_pattern):
    vmem = pl.BlockSpec(memory_space=pltpu.VMEM)
    return pl.pallas_call(
        kernel,
        out_shape=jax.ShapeDtypeStruct((48, 64), F32),
        in_specs=[pl.BlockSpec(memory_space=pl.ANY), vmem, vmem, vmem],
        out_specs=vmem,
        scratch_shapes=[
            pltpu.VMEM((32, 32, 768), BF16),
            pltpu.VMEM((2, 384, 1024), BF16),
            pltpu.VMEM((32, 1536), BF16),
            pltpu.VMEM((NT, NY, NZL, 32, 512), BF16),
            pltpu.VMEM((384, 1536), BF16),
            pltpu.VMEM((1536, 384), BF16),
            pltpu.VMEM((NT, NX, 384, BLOCK), F32),
            pltpu.VMEM((NT, NX, 384, BLOCK), F32),
            pltpu.VMEM((NT, NX, 384, BLOCK), F32),
            pltpu.VMEM((NT, 6, 192, BLOCK), F32),
            pltpu.VMEM((NT, 2, 32, 24, BLOCK), F32),
            pltpu.VMEM((NT, 32, 24, BLOCK), F32),
            pltpu.VMEM((NT, 2, 4, NZL, 24, BLOCK), F32),
            pltpu.VMEM((NT, NZL, 24, BLOCK), F32),
            pltpu.VMEM((NT, NZL, 24, BLOCK), F32),
            pltpu.VMEM((2, 24, BLOCK), F32),
            pltpu.SemaphoreType.DMA,
            pltpu.SemaphoreType.DMA((TOTAL,)),
            pltpu.SemaphoreType.DMA((TOTAL,)),
        ],
        compiler_params=pltpu.CompilerParams(
            collective_id=0, has_side_effects=True, vmem_limit_bytes=48 * 1024 * 1024),
    )(curl_tiles, gradient, a_pattern, g_pattern)


def solution(mesh):
    placed = (P(None, "col", "row"), P(("row", "col"), None), P(), P())
    return jax.shard_map(
        body, mesh=mesh, in_specs=placed, out_specs=P("row", "col"), check_vma=False
    )
```

```python
import jax
import jax.numpy as jnp
from jax import lax
from jax.experimental import pallas as pl
from jax.experimental.pallas import tpu as pltpu
from jax.sharding import PartitionSpec as P

BLOCK = 128
NX, NY, NZL, NZH, NC = 4, 8, 4, 3, 2
NT = 3
F32, BF16 = jnp.float32, jnp.bfloat16
MESH = pl.DeviceIdType.MESH

GATHER = [(0, 0, 256), (0, 256, 256), (1, 0, 256), (1, 256, 256), (2, 0, 256), (2, 256, 256)]
REDUCE = [(0, 0, 1, False, False), (0, 1, 1, False, False), (1, 0, 1, False, False), (1, 1, 1, False, False), (2, 0, 1, True, True), (2, 1, 1, True, True)]

SITES = {}
TOTAL = 0


def site(name, count=1):
    global TOTAL
    SITES[name] = TOTAL
    TOTAL += count


for a in range(len(GATHER)):
    site(("z", a), 4)
    for hop in range(1, 5):
        for side in "RL":
            site(("y", a, hop, side), 2)
for u in range(len(REDUCE)):
    site(("cx", u))
    site(("x", u), 6)
    site(("qc", u))
    site(("q", u), 8)
site("f", 12)
site("gz", 3)
for side in "RL":
    site(("gx", side), 2)


def kernel(a_hbm, g_hbm, ap_hbm, gp_hbm, out_ref, a_buf, g_buf, ap_buf, gp_buf, at, gm, gs, gr, grt, po, pm, cx, xr,
           q, qcr, yr, zr, fin, load_sem, ssem, rsem):
    row, col = lax.axis_index("row"), lax.axis_index("col")
    y, zl = row // NZL, row % NZL
    x, zh, core = col // (NZH * NC), (col // NC) % NZH, col % NC
    sib = 1 - core

    places = {"x": (x, NX), "y": (y, NY), "zl": (zl, NZL), "zh": (zh, NZH)}
    known = {}

    def near(axis, d):
        here, n = places[axis]
        if d % n == 0:
            return here
        if (axis, d % n) not in known:
            known[axis, d % n] = lax.rem(here + d % n, n)
        return known[axis, d % n]

    def at_device(xx, yy, zz, hh, cc):
        return (yy * NZL + zz, xx * (NZH * NC) + hh * NC + cc)

    def dev(dx=0, dy=0, dzl=0, dzh=0, other=False):
        key = (dx % NX, dy % NY, dzl % NZL, dzh % NZH, other)
        if key not in known:
            known[key] = at_device(near("x", dx), near("y", dy), near("zl", dzl), near("zh", dzh), sib if other else core)
        return known[key]

    loads = [pltpu.make_async_copy(src, dst, load_sem.at[i]) for i, (src, dst) in enumerate(
        [(g_hbm, g_buf), (gp_hbm, gp_buf), (ap_hbm, ap_buf), (a_hbm, a_buf)])]
    for load in loads:
        load.start()

    barrier = pltpu.get_barrier_semaphore()
    peers = [dev(dzh=h) for h in range(1, NZH)] + [dev(dzl=i, other=o) for i in range(NZL) for o in (False, True) if i or o]
    peers += [dev(dy=1), dev(dy=-1)] + [dev(dx=d) for d in range(1, NX)]
    for peer in peers:
        pl.semaphore_signal(barrier, inc=1, device_id=peer, device_id_type=MESH)

    drains = []

    def copy_of(name, k, src, dst, to, rk=None):
        i = SITES[name] + k
        return pltpu.make_async_remote_copy(
            src_ref=src, dst_ref=dst, send_sem=ssem.at[i], recv_sem=rsem.at[i if rk is None else SITES[name] + rk],
            device_id=to, device_id_type=MESH)

    def send(name, k, src, dst, to, rk=None):
        copy = copy_of(name, k, src, dst, to, rk)
        copy.start()
        drains.append(copy)

    def arrived(name, k, dst):
        copy_of(name, k, dst, dst, dev(dy=1)).wait_recv()

    def drain():
        while drains:
            drains.pop(0).wait_send()

    loads[0].wait()
    loads[1].wait()
    own_block = row * 6 + col // 4
    lanes = lax.broadcasted_iota(jnp.int32, (12, 192), 1)
    keep = jnp.sum(jnp.where(lanes == own_block, gp_buf[...].astype(F32), 0.0), axis=1, keepdims=True)
    for p in range(12):
        part = slice(p * BLOCK, (p + 1) * BLOCK)
        gm[:, part] = (g_buf[:, part].astype(F32) * jnp.broadcast_to(keep[p:p + 1, :], (32, BLOCK))).astype(BF16)
    me_m = x * NZH + zh
    gr[pl.ds(pl.multiple_of(me_m * 32, 32), 32), :] = gm[...]
    for t in range(NT):
        jj = near("zh", 1 + t)
        blocks = [gm[:, pl.ds(pl.multiple_of(xx * 384 + jj * BLOCK, BLOCK), BLOCK)] for xx in range(NX)]
        gs[t, y, zl] = jnp.concatenate([b[:, h * 64:(h + 1) * 64] for h in range(2) for b in blocks], axis=1)

    pl.semaphore_wait(barrier, len(peers))

    def z_slab(a, zz):
        t, lane, width = GATHER[a]
        return gs.at[t, y, zz, :, pl.ds(lane, width)]

    own_pair = pl.multiple_of(zl // 2 * 2, 2)
    far_pair = pl.multiple_of(2 - own_pair, 2)
    near_step = 3 - 2 * (zl % 2)

    def pair(a, yy, p):
        t, lane, width = GATHER[a]
        return gs.at[t, near("y", yy), pl.ds(far_pair if p else own_pair, 2), :, pl.ds(lane, width)]

    def z0(a):
        for i in (1, 3, 2):
            send(("z", a), i, z_slab(a, zl), z_slab(a, zl), dev(dzl=i))

    def out_y(a, hop, p, right=True, left=True):
        if right and (hop < 4 or p == 0):
            ref = pair(a, 1 - hop, p)
            send(("y", a, hop, "R"), p, ref, ref, dev(dy=1))
        if left and (hop < 4 or p == 1):
            ref = pair(a, hop - 1, p)
            send(("y", a, hop, "L"), p, ref, ref, dev(dy=-1))

    def o1(a, p):
        if p == 0:
            arrived(("z", a), near_step, z_slab(a, zl + 1 - 2 * (zl % 2)))
        else:
            arrived(("z", a), 2, z_slab(a, near("zl", 2)))
            arrived(("z", a), 4 - near_step, z_slab(a, 3 - zl))
        out_y(a, 1, p)

    def fw(a, hop, side, p):
        arrived(("y", a, hop - 1, side), p, pair(a, 1 - hop if side == "R" else hop - 1, p))
        out_y(a, hop, p, right=side == "R", left=side == "L")

    def h5(a):
        arrived(("y", a, 3, "L"), 0, pair(a, 3, 0))
        arrived(("y", a, 3, "R"), 1, pair(a, -3, 1))
        arrived(("y", a, 4, "R"), 0, pair(a, -4, 0))
        arrived(("y", a, 4, "L"), 1, pair(a, 4, 1))

    def prepare_a():
        loads[2].wait()
        loads[3].wait()
        ap = ap_buf[...].astype(F32).astype(BF16)
        want = lax.broadcasted_iota(jnp.int32, (8, 192), 0) + row * 6
        pick = jnp.where(want == lax.broadcasted_iota(jnp.int32, (8, 192), 1), 1.0, 0.0).astype(BF16)
        rows = jnp.dot(pick, ap, preferred_element_type=F32).astype(BF16)
        want = (lax.broadcasted_iota(jnp.int32, (192, 1024), 1) // 32) * 6 + col // 4
        pick = jnp.where(want == lax.broadcasted_iota(jnp.int32, (192, 1024), 0), 1.0, 0.0).astype(BF16)
        mask = jnp.dot(rows, pick, preferred_element_type=F32)
        for b in range(6):
            block = a_buf[:, :, b * BLOCK:(b + 1) * BLOCK].reshape(1024, BLOCK)
            turned = (block.T.astype(F32) * mask[b:b + 1, :]).astype(BF16)
            for i in range(4):
                at[i % 2, (2 * b + i // 2) * 32:(2 * b + i // 2 + 1) * 32, :] = turned[i * 32:(i + 1) * 32]

    def g0():
        own = gr.at[pl.ds(pl.multiple_of(me_m * 32, 32), 32)]
        for h in range(1, NZH):
            send("gz", h, own, own, dev(dzh=h))

    def gx_rows(dx, first=0, count=96):
        return gr.at[pl.ds(pl.multiple_of(near("x", dx) * 96 + first, 16), count)]

    def g1():
        for h in range(1, NZH):
            m = x * NZH + near("zh", -h)
            arrived("gz", h, gr.at[pl.ds(pl.multiple_of(m * 32, 32), 32)])
        send(("gx", "R"), 0, gx_rows(0), gx_rows(0), dev(dx=1))
        send(("gx", "L"), 0, gx_rows(0), gx_rows(0), dev(dx=-1))

    def g2():
        arrived(("gx", "R"), 0, gx_rows(-1))
        send(("gx", "R"), 1, gx_rows(-1, 0, 48), gx_rows(-1, 0, 48), dev(dx=1))
        arrived(("gx", "L"), 0, gx_rows(1))
        send(("gx", "L"), 1, gx_rows(1, 48, 48), gx_rows(1, 48, 48), dev(dx=-1))

    def g3():
        arrived(("gx", "R"), 1, gx_rows(-2, 0, 48))
        arrived(("gx", "L"), 1, gx_rows(2, 48, 48))
        for b in range(3):
            part = slice(b * BLOCK, (b + 1) * BLOCK)
            grt[:, part] = gr[part, :].T

    def halves(u):
        return REDUCE[u][0], range(REDUCE[u][1], REDUCE[u][1] + REDUCE[u][2]), pl.ds(REDUCE[u][1], REDUCE[u][2])

    def s0(u):
        t, hs, ds = halves(u)
        for half, out in ((sib, po), (core, pm)):
            for h in hs:
                b = gs[t, :, :, :, h * 256:(h + 1) * 256].reshape(1024, 256)
                r = jnp.dot(at[half], b, preferred_element_type=F32)
                for xx in range(NX):
                    part = r[:, xx * 64:(xx + 1) * 64]
                    out[t, h, xx] = jnp.concatenate([part[:192], part[192:]], axis=1)
            if out is po:
                send(("cx", u), 0, po.at[t, ds], cx.at[t, ds], dev(other=True))

    xp, xm, xo = near("x", 1), near("x", -1), near("x", 2)
    A, B, ALL = pl.ds(0, 96), pl.ds(96, 96), pl.ds(0, 192)

    def s1(u):
        t, hs, ds = halves(u)
        arrived(("cx", u), 0, cx.at[t, ds])
        name = ("x", u)

        def add(xx):
            for h in hs:
                pm[t, h, xx] += cx[t, h, xx]

        add(xo)
        if REDUCE[u][3]:
            send(name, 0, pm.at[t, ds, xo], xr.at[t, ds, 0], dev(dx=2))
            add(xp)
            send(name, 1, pm.at[t, ds, xp], xr.at[t, ds, 1], dev(dx=1))
            add(xm)
            send(name, 2, pm.at[t, ds, xm], xr.at[t, ds, 2], dev(dx=-1))
        else:
            send(name, 0, pm.at[t, ds, xo, A], xr.at[t, ds, 0, A], dev(dx=1))
            send(name, 3, pm.at[t, ds, xo, B], xr.at[t, ds, 0, B], dev(dx=-1))
            add(xp)
            send(name, 1, pm.at[t, ds, xp, B], xr.at[t, ds, 1, B], dev(dx=1))
            add(xm)
            send(name, 4, pm.at[t, ds, xm, A], xr.at[t, ds, 2, A], dev(dx=-1))
        add(x)

    def s2(u):
        t, hs, ds = halves(u)
        name = ("x", u)
        arrived(name, 0, xr.at[t, ds, 0, A])
        for h in hs:
            pm[t, h, xp, A] += xr[t, h, 0, A]
        send(name, 2, pm.at[t, ds, xp, A], xr.at[t, ds, 1, A], dev(dx=1))
        arrived(name, 3, xr.at[t, ds, 0, B])
        for h in hs:
            pm[t, h, xm, B] += xr[t, h, 0, B]
        send(name, 5, pm.at[t, ds, xm, B], xr.at[t, ds, 2, B], dev(dx=-1))

    def s3(u):
        t, hs, ds = halves(u)
        name = ("x", u)
        if REDUCE[u][3]:
            for k in range(3):
                arrived(name, k, xr.at[t, ds, k])
        else:
            arrived(name, 1, xr.at[t, ds, 1, B])
            arrived(name, 4, xr.at[t, ds, 2, A])
            arrived(name, 2, xr.at[t, ds, 1, A])
            arrived(name, 5, xr.at[t, ds, 2, B])
        pieces = []
        for h in hs:
            total = pm[t, h, x] + (xr[t, h, 1] + xr[t, h, 2])
            if REDUCE[u][3]:
                total = total + xr[t, h, 0]
            total = jnp.concatenate([total[:, :64], total[:, 64:]], axis=0)
            high = total.astype(BF16)
            pieces += [high, (total - high.astype(F32)).astype(BF16)]
        r = jnp.dot(grt[...], jnp.concatenate(pieces, axis=1), preferred_element_type=F32)
        for n, h in enumerate(hs):
            v = (r[:, n * BLOCK:n * BLOCK + 64] + r[:, n * BLOCK + 64:(n + 1) * BLOCK]).reshape(32, 2, 24, 64)
            v = jnp.concatenate([v[:, 0], v[:, 1]], axis=2).reshape(NY, NC, 2, 24, BLOCK)
            for k in range(NC):
                q[t, h, k] = v[:, k]
        send(("qc", u), 0, q.at[t, ds, sib], qcr.at[t, ds], dev(other=True))

    def q_to(u, dy, p=None):
        t, hs, ds = halves(u)
        return q.at[t, ds, core, near("y", dy), pl.ds(0, 2) if p is None else pl.ds(p, 1)]

    def y_slot(u, k, p=None):
        t, hs, ds = halves(u)
        return yr.at[t, ds, k, pl.ds(0, 2) if p is None else pl.ds(p, 1)]

    def s4(u):
        t, hs, ds = halves(u)
        arrived(("qc", u), 0, qcr.at[t, ds])
        for h in hs:
            q[t, h, core] += qcr[t, h]
        if REDUCE[u][4]:
            for d in (4, 3, 5, 2, 6, 1, 7):
                send(("q", u), d, q_to(u, d), y_slot(u, d), dev(dy=d))
        else:
            send(("q", u), 0, q_to(u, 4, 0), y_slot(u, 0, 0), dev(dy=1))
            send(("q", u), 4, q_to(u, -4, 1), y_slot(u, 4, 1), dev(dy=-1))

    def y_step(u, k):
        if REDUCE[u][4]:
            return
        for side, sign in ((0, 1), (1, -1)):
            p = side if k == 1 else None
            slot = y_slot(u, 4 * side + k - 1, p)
            arrived(("q", u), 4 * side + k - 1, slot)
            own = q_to(u, sign * (4 - k), p)
            own[...] += slot[...]
            send(("q", u), 4 * side + k, q_to(u, sign * (4 - k)), y_slot(u, 4 * side + k), dev(dy=sign))

    def s5(u):
        y_step(u, 1)

    def s6(u):
        y_step(u, 2)

    def s7(u):
        y_step(u, 3)

    def s8(u):
        t, hs, ds = halves(u)
        slots = range(1, 8) if REDUCE[u][4] else (3, 7)
        for k in slots:
            arrived(("q", u), k, y_slot(u, k))
        for h in hs:
            total = q[t, h, core, y]
            for k in slots:
                total = total + yr[t, h, k]
            fin[t, h] = total
            for b in range(2):
                last = f_copy(t, h, b)
                if t < 2:
                    last.start()
                else:
                    mine = f_mine(h, b)
                    pl.when(jnp.logical_not(mine))(last.start)

                    @pl.when(mine)
                    def _():
                        zr[2, 0] = fin[2, h, b]

    def f_mine(h, b):
        return jnp.logical_and(zl == 2 * core + b, core == h)

    def f_copy(t, h, b):
        zz = 2 * core + b
        i = lax.rem(zz - zl + NZL, NZL)
        return copy_of("f", t * 4 + h * 2 + b, fin.at[t, h, b], zr.at[t, i],
                       at_device(x, y, zz, near("zh", t + 1), h), rk=t * 4 + i)

    def finish():
        for t in range(NT):
            for i in range(NZL):
                def wait(t=t, i=i):
                    arrived("f", t * 4 + i, zr.at[t, i])
                if t < 2 or i:
                    wait()
                else:
                    pl.when(core != zl // 2)(wait)
        total = zr[0, 0]
        for n in range(1, 12):
            total = total + zr[n // 4, n % 4]
        out_ref[0:24, :] = total[:, :64]
        out_ref[24:48, :] = total[:, 64:]
        for t in range(NT):
            for h in range(NC):
                for b in range(2):
                    last = f_copy(t, h, b)
                    if t < 2:
                        last.wait_send()
                    else:
                        pl.when(jnp.logical_not(f_mine(h, b)))(last.wait_send)

    z0(0)
    prepare_a()
    z0(1)
    z0(2)
    g0()
    z0(3)
    z0(4)
    z0(5)
    o1(0,0)
    o1(1,0)
    o1(0,1)
    o1(2,0)
    o1(1,1)
    fw(0,2,"R",0)
    fw(0,2,"L",0)
    o1(2,1)
    fw(1,2,"R",0)
    fw(1,2,"L",0)
    fw(0,2,"R",1)
    fw(0,2,"L",1)
    fw(2,2,"R",0)
    fw(2,2,"L",0)
    fw(1,2,"R",1)
    fw(1,2,"L",1)
    fw(0,3,"R",0)
    fw(0,3,"L",0)
    fw(2,2,"R",1)
    fw(2,2,"L",1)
    fw(1,3,"R",0)
    fw(1,3,"L",0)
    fw(0,3,"R",1)
    fw(0,3,"L",1)
    fw(2,3,"R",0)
    fw(2,3,"L",0)
    fw(1,3,"R",1)
    fw(1,3,"L",1)
    fw(0,4,"R",0)
    o1(3,0)
    fw(2,3,"R",1)
    fw(2,3,"L",1)
    o1(4,0)
    fw(1,4,"R",0)
    g1()
    o1(3,1)
    fw(0,4,"L",1)
    o1(5,0)
    fw(2,4,"R",0)
    o1(4,1)
    fw(1,4,"L",1)
    o1(5,1)
    fw(3,2,"L",0)
    fw(3,2,"R",0)
    fw(2,4,"L",1)
    fw(4,2,"L",0)
    fw(4,2,"R",0)
    fw(3,2,"L",1)
    h5(0)
    s0(0)
    fw(3,2,"R",1)
    fw(5,2,"L",0)
    fw(5,2,"R",0)
    fw(4,2,"L",1)
    h5(1)
    s0(1)
    s1(0)
    fw(3,3,"L",0)
    g2()
    fw(4,2,"R",1)
    h5(2)
    fw(3,3,"R",0)
    s0(2)
    s1(1)
    fw(3,3,"L",1)
    fw(3,3,"R",1)
    fw(4,3,"R",0)
    fw(4,3,"L",0)
    fw(5,2,"L",1)
    fw(5,3,"L",0)
    fw(5,3,"R",0)
    s2(0)
    s1(2)
    fw(3,4,"R",0)
    fw(4,3,"R",1)
    fw(4,3,"L",1)
    fw(5,2,"R",1)
    fw(3,4,"L",1)
    fw(4,4,"R",0)
    fw(5,3,"L",1)
    fw(5,4,"R",0)
    g3()
    fw(4,4,"L",1)
    s2(1)
    h5(3)
    s0(3)
    fw(5,3,"R",1)
    fw(5,4,"L",1)
    s3(0)
    s1(3)
    s2(2)
    h5(4)
    s4(0)
    s0(4)
    s3(1)
    h5(5)
    s0(5)
    s2(3)
    s5(0)
    s4(1)
    s1(4)
    s1(5)
    s3(2)
    s6(0)
    s5(1)
    s3(3)
    s4(2)
    s4(3)
    s7(0)
    s6(1)
    s3(4)
    s5(2)
    s5(3)
    s4(4)
    s8(0)
    s7(1)
    s3(5)
    s6(2)
    s6(3)
    s4(5)
    s8(4)
    s8(1)
    s7(2)
    s7(3)
    s8(5)
    s8(2)
    s8(3)
    finish()
    drain()


def body(curl_tiles, gradient, a_pattern, g_pattern):
    hbm = pl.BlockSpec(memory_space=pl.ANY)
    return pl.pallas_call(
        kernel,
        out_shape=jax.ShapeDtypeStruct((48, 64), F32),
        in_specs=[hbm] * 4,
        out_specs=pl.BlockSpec(memory_space=pltpu.VMEM),
        scratch_shapes=[
            pltpu.VMEM((32, 32, 768), BF16),
            pltpu.VMEM((32, 1536), BF16),
            pltpu.VMEM((192, 192), jnp.int32),
            pltpu.VMEM((12, 192), jnp.int32),
            pltpu.VMEM((2, 384, 1024), BF16),
            pltpu.VMEM((32, 1536), BF16),
            pltpu.VMEM((NT, NY, NZL, 32, 512), BF16),
            pltpu.VMEM((384, 1536), BF16),
            pltpu.VMEM((1536, 384), BF16),
            pltpu.VMEM((NT, 2, NX, 192, BLOCK), F32),
            pltpu.VMEM((NT, 2, NX, 192, BLOCK), F32),
            pltpu.VMEM((NT, 2, NX, 192, BLOCK), F32),
            pltpu.VMEM((NT, 2, 3, 192, BLOCK), F32),
            pltpu.VMEM((NT, 2, NC, NY, 2, 24, BLOCK), F32),
            pltpu.VMEM((NT, 2, NY, 2, 24, BLOCK), F32),
            pltpu.VMEM((NT, 2, 8, 2, 24, BLOCK), F32),
            pltpu.VMEM((NT, NZL, 24, BLOCK), F32),
            pltpu.VMEM((NT, 2, 2, 24, BLOCK), F32),
            pltpu.SemaphoreType.DMA((4,)),
            pltpu.SemaphoreType.DMA((TOTAL,)),
            pltpu.SemaphoreType.DMA((TOTAL,)),
        ],
        compiler_params=pltpu.CompilerParams(
            collective_id=0, has_side_effects=True, vmem_limit_bytes=60 * 1024 * 1024),
    )(curl_tiles, gradient, a_pattern, g_pattern.T)


def solution(mesh):
    placed = (P(None, "col", "row"), P(("row", "col"), None), P(), P())
    return jax.shard_map(
        body, mesh=mesh, in_specs=placed, out_specs=P("row", "col"), check_vma=False
    )
```

```python
import jax
import jax.numpy as jnp
from jax import lax
from jax.experimental import pallas as pl
from jax.experimental.pallas import tpu as pltpu
from jax.sharding import PartitionSpec as P

BLOCK = 128
NX, NY, NZL, NZH, NC = 4, 8, 4, 3, 2
NT = 3
F32, BF16 = jnp.float32, jnp.bfloat16
MESH = pl.DeviceIdType.MESH

GATHER = [(0, 0, 256), (0, 256, 256), (1, 0, 256), (1, 256, 256), (2, 0, 256), (2, 256, 256)]
REDUCE = [(0, 0, 1, False, False), (0, 1, 1, False, False), (1, 0, 1, False, False), (1, 1, 1, False, False), (2, 0, 1, True, True), (2, 1, 1, True, True)]

SITES = {}
TOTAL = 0


def site(name, count=1):
    global TOTAL
    SITES[name] = TOTAL
    TOTAL += count


for a in range(len(GATHER)):
    site(("z", a), 4)
    for hop in range(1, 5):
        for side in "RL":
            site(("y", a, hop, side), 2)
for u in range(len(REDUCE)):
    site(("cx", u))
    site(("x", u), 6)
    site(("qc", u))
    site(("q", u), 8)
site("f", 12)
site("gz", 3)
for side in "RL":
    site(("gx", side), 2)


def kernel(a_hbm, g_hbm, ap_hbm, gp_hbm, out_ref, a_buf, g_buf, ap_buf, gp_buf, at, gm, gs, gr, grt, po, pm, cx, xr,
           q, qcr, yr, zr, fin, load_sem, ssem, rsem):
    row, col = lax.axis_index("row"), lax.axis_index("col")
    y, zl = row // NZL, row % NZL
    x, zh, core = col // (NZH * NC), (col // NC) % NZH, col % NC
    sib = 1 - core

    places = {"x": (x, NX), "y": (y, NY), "zl": (zl, NZL), "zh": (zh, NZH)}
    known = {}

    def near(axis, d):
        here, n = places[axis]
        if d % n == 0:
            return here
        if (axis, d % n) not in known:
            known[axis, d % n] = lax.rem(here + d % n, n)
        return known[axis, d % n]

    def at_device(xx, yy, zz, hh, cc):
        return (yy * NZL + zz, xx * (NZH * NC) + hh * NC + cc)

    def dev(dx=0, dy=0, dzl=0, dzh=0, other=False):
        key = (dx % NX, dy % NY, dzl % NZL, dzh % NZH, other)
        if key not in known:
            known[key] = at_device(near("x", dx), near("y", dy), near("zl", dzl), near("zh", dzh), sib if other else core)
        return known[key]

    loads = [pltpu.make_async_copy(src, dst, load_sem.at[i]) for i, (src, dst) in enumerate(
        [(g_hbm, g_buf), (gp_hbm, gp_buf), (ap_hbm, ap_buf), (a_hbm, a_buf)])]
    for load in loads:
        load.start()

    barrier = pltpu.get_barrier_semaphore()
    peers = [dev(dzh=h) for h in range(1, NZH)] + [dev(dzl=i, other=o) for i in range(NZL) for o in (False, True) if i or o]
    peers += [dev(dy=1), dev(dy=-1)] + [dev(dx=d) for d in range(1, NX)]
    for peer in peers:
        pl.semaphore_signal(barrier, inc=1, device_id=peer, device_id_type=MESH)

    drains = []

    def copy_of(name, k, src, dst, to, rk=None):
        i = SITES[name] + k
        return pltpu.make_async_remote_copy(
            src_ref=src, dst_ref=dst, send_sem=ssem.at[i], recv_sem=rsem.at[i if rk is None else SITES[name] + rk],
            device_id=to, device_id_type=MESH)

    def send(name, k, src, dst, to, rk=None):
        copy = copy_of(name, k, src, dst, to, rk)
        copy.start()
        drains.append(copy)

    def arrived(name, k, dst):
        copy_of(name, k, dst, dst, dev(dy=1)).wait_recv()

    def drain():
        while drains:
            drains.pop(0).wait_send()

    loads[0].wait()
    loads[1].wait()
    own_block = row * 6 + col // 4
    lanes = lax.broadcasted_iota(jnp.int32, (12, 192), 1)
    keep = jnp.sum(jnp.where(lanes == own_block, gp_buf[...].astype(F32), 0.0), axis=1, keepdims=True)
    for p in range(12):
        part = slice(p * BLOCK, (p + 1) * BLOCK)
        gm[:, part] = (g_buf[:, part].astype(F32) * jnp.broadcast_to(keep[p:p + 1, :], (32, BLOCK))).astype(BF16)
    me_m = x * NZH + zh
    gr[pl.ds(pl.multiple_of(me_m * 32, 32), 32), :] = gm[...]
    for t in range(NT):
        jj = near("zh", 1 + t)
        blocks = [gm[:, pl.ds(pl.multiple_of(xx * 384 + jj * BLOCK, BLOCK), BLOCK)] for xx in range(NX)]
        gs[t, y, zl] = jnp.concatenate([b[:, h * 64:(h + 1) * 64] for h in range(2) for b in blocks], axis=1)

    pl.semaphore_wait(barrier, len(peers))

    def z_slab(a, zz):
        t, lane, width = GATHER[a]
        return gs.at[t, y, zz, :, pl.ds(lane, width)]

    own_pair = pl.multiple_of(zl // 2 * 2, 2)
    far_pair = pl.multiple_of(2 - own_pair, 2)
    near_step = 3 - 2 * (zl % 2)

    def pair(a, yy, p):
        t, lane, width = GATHER[a]
        return gs.at[t, near("y", yy), pl.ds(far_pair if p else own_pair, 2), :, pl.ds(lane, width)]

    def z0(a):
        for i in (1, 3, 2):
            send(("z", a), i, z_slab(a, zl), z_slab(a, zl), dev(dzl=i))

    def out_y(a, hop, p, right=True, left=True):
        if right and (hop < 4 or p == 0):
            ref = pair(a, 1 - hop, p)
            send(("y", a, hop, "R"), p, ref, ref, dev(dy=1))
        if left and (hop < 4 or p == 1):
            ref = pair(a, hop - 1, p)
            send(("y", a, hop, "L"), p, ref, ref, dev(dy=-1))

    def o1(a, p):
        if p == 0:
            arrived(("z", a), near_step, z_slab(a, zl + 1 - 2 * (zl % 2)))
        else:
            arrived(("z", a), 2, z_slab(a, near("zl", 2)))
            arrived(("z", a), 4 - near_step, z_slab(a, 3 - zl))
        out_y(a, 1, p)

    def fw(a, hop, side, p):
        arrived(("y", a, hop - 1, side), p, pair(a, 1 - hop if side == "R" else hop - 1, p))
        out_y(a, hop, p, right=side == "R", left=side == "L")

    def h5(a):
        arrived(("y", a, 3, "L"), 0, pair(a, 3, 0))
        arrived(("y", a, 3, "R"), 1, pair(a, -3, 1))
        arrived(("y", a, 4, "R"), 0, pair(a, -4, 0))
        arrived(("y", a, 4, "L"), 1, pair(a, 4, 1))

    def prepare_a():
        loads[2].wait()
        loads[3].wait()
        ap = ap_buf[...].astype(F32).astype(BF16)
        want = lax.broadcasted_iota(jnp.int32, (8, 192), 0) + row * 6
        pick = jnp.where(want == lax.broadcasted_iota(jnp.int32, (8, 192), 1), 1.0, 0.0).astype(BF16)
        rows = jnp.dot(pick, ap, preferred_element_type=F32).astype(BF16)
        want = (lax.broadcasted_iota(jnp.int32, (192, 1024), 1) // 32) * 6 + col // 4
        pick = jnp.where(want == lax.broadcasted_iota(jnp.int32, (192, 1024), 0), 1.0, 0.0).astype(BF16)
        mask = jnp.dot(rows, pick, preferred_element_type=F32)
        for b in range(6):
            block = a_buf[:, :, b * BLOCK:(b + 1) * BLOCK].reshape(1024, BLOCK)
            turned = (block.T.astype(F32) * mask[b:b + 1, :]).astype(BF16)
            for i in range(4):
                at[i % 2, (2 * b + i // 2) * 32:(2 * b + i // 2 + 1) * 32, :] = turned[i * 32:(i + 1) * 32]

    def g0():
        own = gr.at[pl.ds(pl.multiple_of(me_m * 32, 32), 32)]
        for h in range(1, NZH):
            send("gz", h, own, own, dev(dzh=h))

    def gx_rows(dx, first=0, count=96):
        return gr.at[pl.ds(pl.multiple_of(near("x", dx) * 96 + first, 16), count)]

    def g1():
        for h in range(1, NZH):
            m = x * NZH + near("zh", -h)
            arrived("gz", h, gr.at[pl.ds(pl.multiple_of(m * 32, 32), 32)])
        send(("gx", "R"), 0, gx_rows(0), gx_rows(0), dev(dx=1))
        send(("gx", "L"), 0, gx_rows(0), gx_rows(0), dev(dx=-1))

    def g2():
        arrived(("gx", "R"), 0, gx_rows(-1))
        send(("gx", "R"), 1, gx_rows(-1, 0, 48), gx_rows(-1, 0, 48), dev(dx=1))
        arrived(("gx", "L"), 0, gx_rows(1))
        send(("gx", "L"), 1, gx_rows(1, 48, 48), gx_rows(1, 48, 48), dev(dx=-1))

    def g3():
        arrived(("gx", "R"), 1, gx_rows(-2, 0, 48))
        arrived(("gx", "L"), 1, gx_rows(2, 48, 48))
        for b in range(3):
            part = slice(b * BLOCK, (b + 1) * BLOCK)
            grt[:, part] = gr[part, :].T

    def halves(u):
        return REDUCE[u][0], range(REDUCE[u][1], REDUCE[u][1] + REDUCE[u][2]), pl.ds(REDUCE[u][1], REDUCE[u][2])

    def s0(u):
        t, hs, ds = halves(u)
        for half, out in ((sib, po), (core, pm)):
            for h in hs:
                b = gs[t, :, :, :, h * 256:(h + 1) * 256].reshape(1024, 256)
                r = jnp.dot(at[half], b, preferred_element_type=F32)
                for xx in range(NX):
                    part = r[:, xx * 64:(xx + 1) * 64]
                    out[t, h, xx] = jnp.concatenate([part[:192], part[192:]], axis=1)
            if out is po:
                send(("cx", u), 0, po.at[t, ds], cx.at[t, ds], dev(other=True))

    xp, xm, xo = near("x", 1), near("x", -1), near("x", 2)
    A, B, ALL = pl.ds(0, 96), pl.ds(96, 96), pl.ds(0, 192)

    def s1(u):
        t, hs, ds = halves(u)
        arrived(("cx", u), 0, cx.at[t, ds])
        name = ("x", u)

        def add(xx):
            for h in hs:
                pm[t, h, xx] += cx[t, h, xx]

        add(xo)
        if REDUCE[u][3]:
            send(name, 0, pm.at[t, ds, xo], xr.at[t, ds, 0], dev(dx=2))
            add(xp)
            send(name, 1, pm.at[t, ds, xp], xr.at[t, ds, 1], dev(dx=1))
            add(xm)
            send(name, 2, pm.at[t, ds, xm], xr.at[t, ds, 2], dev(dx=-1))
        else:
            send(name, 0, pm.at[t, ds, xo, A], xr.at[t, ds, 0, A], dev(dx=1))
            send(name, 3, pm.at[t, ds, xo, B], xr.at[t, ds, 0, B], dev(dx=-1))
            add(xp)
            send(name, 1, pm.at[t, ds, xp, B], xr.at[t, ds, 1, B], dev(dx=1))
            add(xm)
            send(name, 4, pm.at[t, ds, xm, A], xr.at[t, ds, 2, A], dev(dx=-1))
        add(x)

    def s2(u):
        t, hs, ds = halves(u)
        name = ("x", u)
        arrived(name, 0, xr.at[t, ds, 0, A])
        for h in hs:
            pm[t, h, xp, A] += xr[t, h, 0, A]
        send(name, 2, pm.at[t, ds, xp, A], xr.at[t, ds, 1, A], dev(dx=1))
        arrived(name, 3, xr.at[t, ds, 0, B])
        for h in hs:
            pm[t, h, xm, B] += xr[t, h, 0, B]
        send(name, 5, pm.at[t, ds, xm, B], xr.at[t, ds, 2, B], dev(dx=-1))

    def s3(u):
        t, hs, ds = halves(u)
        name = ("x", u)
        if REDUCE[u][3]:
            for k in range(3):
                arrived(name, k, xr.at[t, ds, k])
        else:
            arrived(name, 1, xr.at[t, ds, 1, B])
            arrived(name, 4, xr.at[t, ds, 2, A])
            arrived(name, 2, xr.at[t, ds, 1, A])
            arrived(name, 5, xr.at[t, ds, 2, B])
        pieces = []
        for h in hs:
            total = pm[t, h, x] + (xr[t, h, 1] + xr[t, h, 2])
            if REDUCE[u][3]:
                total = total + xr[t, h, 0]
            total = jnp.concatenate([total[:, :64], total[:, 64:]], axis=0)
            high = total.astype(BF16)
            pieces += [high, (total - high.astype(F32)).astype(BF16)]
        r = jnp.dot(grt[...], jnp.concatenate(pieces, axis=1), preferred_element_type=F32)
        for n, h in enumerate(hs):
            v = (r[:, n * BLOCK:n * BLOCK + 64] + r[:, n * BLOCK + 64:(n + 1) * BLOCK]).reshape(32, 2, 24, 64)
            v = jnp.concatenate([v[:, 0], v[:, 1]], axis=2).reshape(NY, NC, 2, 24, BLOCK)
            for k in range(NC):
                q[t, h, k] = v[:, k]
        send(("qc", u), 0, q.at[t, ds, sib], qcr.at[t, ds], dev(other=True))

    def q_to(u, dy, p=None):
        t, hs, ds = halves(u)
        return q.at[t, ds, core, near("y", dy), pl.ds(0, 2) if p is None else pl.ds(p, 1)]

    def y_slot(u, k, p=None):
        t, hs, ds = halves(u)
        return yr.at[t, ds, k, pl.ds(0, 2) if p is None else pl.ds(p, 1)]

    def s4(u):
        t, hs, ds = halves(u)
        arrived(("qc", u), 0, qcr.at[t, ds])
        for h in hs:
            q[t, h, core] += qcr[t, h]
        if REDUCE[u][4]:
            for d in (4, 3, 5, 2, 6, 1, 7):
                send(("q", u), d, q_to(u, d), y_slot(u, d), dev(dy=d))
        else:
            send(("q", u), 0, q_to(u, 4, 0), y_slot(u, 0, 0), dev(dy=1))
            send(("q", u), 4, q_to(u, -4, 1), y_slot(u, 4, 1), dev(dy=-1))

    def y_step(u, k):
        if REDUCE[u][4]:
            return
        for side, sign in ((0, 1), (1, -1)):
            p = side if k == 1 else None
            slot = y_slot(u, 4 * side + k - 1, p)
            arrived(("q", u), 4 * side + k - 1, slot)
            own = q_to(u, sign * (4 - k), p)
            own[...] += slot[...]
            send(("q", u), 4 * side + k, q_to(u, sign * (4 - k)), y_slot(u, 4 * side + k), dev(dy=sign))

    def s5(u):
        y_step(u, 1)

    def s6(u):
        y_step(u, 2)

    def s7(u):
        y_step(u, 3)

    def s8(u):
        t, hs, ds = halves(u)
        slots = range(1, 8) if REDUCE[u][4] else (3, 7)
        for k in slots:
            arrived(("q", u), k, y_slot(u, k))
        for h in hs:
            total = q[t, h, core, y]
            for k in slots:
                total = total + yr[t, h, k]
            fin[t, h] = total
            for b in range(2):
                last = f_copy(t, h, b)
                if t < 2:
                    last.start()
                else:
                    mine = f_mine(h, b)
                    pl.when(jnp.logical_not(mine))(last.start)

                    @pl.when(mine)
                    def _():
                        zr[2, 0] = fin[2, h, b]

    def f_mine(h, b):
        return jnp.logical_and(zl == 2 * core + b, core == h)

    def f_copy(t, h, b):
        zz = 2 * core + b
        i = lax.rem(zz - zl + NZL, NZL)
        return copy_of("f", t * 4 + h * 2 + b, fin.at[t, h, b], zr.at[t, i],
                       at_device(x, y, zz, near("zh", t + 1), h), rk=t * 4 + i)

    def finish():
        for t in range(NT):
            for i in range(NZL):
                def wait(t=t, i=i):
                    arrived("f", t * 4 + i, zr.at[t, i])
                if t < 2 or i:
                    wait()
                else:
                    pl.when(core != zl // 2)(wait)
        total = zr[0, 0]
        for n in range(1, 12):
            total = total + zr[n // 4, n % 4]
        out_ref[0:24, :] = total[:, :64]
        out_ref[24:48, :] = total[:, 64:]
        for t in range(NT):
            for h in range(NC):
                for b in range(2):
                    last = f_copy(t, h, b)
                    if t < 2:
                        last.wait_send()
                    else:
                        pl.when(jnp.logical_not(f_mine(h, b)))(last.wait_send)

    z0(0)
    prepare_a()
    z0(1)
    z0(2)
    g0()
    z0(3)
    z0(4)
    z0(5)
    o1(0,0)
    o1(0,1)
    o1(1,0)
    o1(1,1)
    fw(0,2,"R",0)
    fw(0,2,"L",0)
    fw(0,2,"R",1)
    fw(0,2,"L",1)
    fw(1,2,"R",0)
    fw(1,2,"L",0)
    fw(1,2,"R",1)
    fw(1,2,"L",1)
    o1(2,0)
    o1(2,1)
    fw(0,3,"R",0)
    fw(0,3,"L",0)
    fw(0,3,"R",1)
    fw(0,3,"L",1)
    fw(1,3,"R",0)
    fw(1,3,"L",0)
    fw(1,3,"R",1)
    fw(1,3,"L",1)
    fw(2,2,"R",0)
    fw(2,2,"L",0)
    fw(2,2,"R",1)
    fw(2,2,"L",1)
    o1(3,0)
    fw(0,4,"R",0)
    fw(0,4,"L",1)
    g1()
    fw(1,4,"R",0)
    o1(3,1)
    o1(5,0)
    fw(1,4,"L",1)
    fw(2,3,"R",0)
    fw(2,3,"L",0)
    fw(2,3,"R",1)
    fw(2,3,"L",1)
    o1(5,1)
    fw(3,2,"R",0)
    fw(3,2,"L",0)
    h5(0)
    s0(0)
    fw(3,2,"L",1)
    fw(3,2,"R",1)
    fw(5,2,"L",0)
    fw(5,2,"R",0)
    h5(1)
    s0(1)
    fw(2,4,"R",0)
    s1(0)
    fw(2,4,"L",1)
    fw(5,2,"R",1)
    fw(5,2,"L",1)
    s1(1)
    fw(3,3,"L",0)
    g2()
    fw(3,3,"R",0)
    fw(3,3,"R",1)
    fw(3,3,"L",1)
    o1(4,0)
    o1(4,1)
    fw(5,3,"R",0)
    fw(5,3,"L",0)
    s2(0)
    h5(2)
    s0(2)
    fw(5,3,"R",1)
    fw(5,3,"L",1)
    fw(3,4,"R",0)
    s2(1)
    fw(3,4,"L",1)
    s1(2)
    fw(4,2,"L",0)
    fw(4,2,"R",0)
    fw(4,2,"R",1)
    fw(4,2,"L",1)
    fw(5,4,"R",0)
    fw(5,4,"L",1)
    h5(3)
    s0(3)
    g3()
    fw(4,3,"L",0)
    fw(4,3,"R",0)
    fw(4,3,"R",1)
    s3(0)
    fw(4,3,"L",1)
    s1(3)
    s3(1)
    s4(0)
    s2(2)
    h5(5)
    s0(5)
    fw(4,4,"R",0)
    s4(1)
    fw(4,4,"L",1)
    s2(3)
    s1(5)
    s5(0)
    s5(1)
    s3(2)
    h5(4)
    s0(4)
    s3(3)
    s6(0)
    s4(2)
    s6(1)
    s1(4)
    s4(3)
    s7(0)
    s5(2)
    s3(5)
    s7(1)
    s5(3)
    s4(5)
    s8(0)
    s6(2)
    s8(1)
    s3(4)
    s6(3)
    s4(4)
    s8(5)
    s7(2)
    s7(3)
    s8(4)
    s8(2)
    s8(3)
    finish()
    drain()


def body(curl_tiles, gradient, a_pattern, g_pattern):
    hbm = pl.BlockSpec(memory_space=pl.ANY)
    return pl.pallas_call(
        kernel,
        out_shape=jax.ShapeDtypeStruct((48, 64), F32),
        in_specs=[hbm] * 4,
        out_specs=pl.BlockSpec(memory_space=pltpu.VMEM),
        scratch_shapes=[
            pltpu.VMEM((32, 32, 768), BF16),
            pltpu.VMEM((32, 1536), BF16),
            pltpu.VMEM((192, 192), jnp.int32),
            pltpu.VMEM((12, 192), jnp.int32),
            pltpu.VMEM((2, 384, 1024), BF16),
            pltpu.VMEM((32, 1536), BF16),
            pltpu.VMEM((NT, NY, NZL, 32, 512), BF16),
            pltpu.VMEM((384, 1536), BF16),
            pltpu.VMEM((1536, 384), BF16),
            pltpu.VMEM((NT, 2, NX, 192, BLOCK), F32),
            pltpu.VMEM((NT, 2, NX, 192, BLOCK), F32),
            pltpu.VMEM((NT, 2, NX, 192, BLOCK), F32),
            pltpu.VMEM((NT, 2, 3, 192, BLOCK), F32),
            pltpu.VMEM((NT, 2, NC, NY, 2, 24, BLOCK), F32),
            pltpu.VMEM((NT, 2, NY, 2, 24, BLOCK), F32),
            pltpu.VMEM((NT, 2, 8, 2, 24, BLOCK), F32),
            pltpu.VMEM((NT, NZL, 24, BLOCK), F32),
            pltpu.VMEM((NT, 2, 2, 24, BLOCK), F32),
            pltpu.SemaphoreType.DMA((4,)),
            pltpu.SemaphoreType.DMA((TOTAL,)),
            pltpu.SemaphoreType.DMA((TOTAL,)),
        ],
        compiler_params=pltpu.CompilerParams(
            collective_id=0, has_side_effects=True, vmem_limit_bytes=60 * 1024 * 1024),
    )(curl_tiles, gradient, a_pattern, g_pattern.T)


def solution(mesh):
    placed = (P(None, "col", "row"), P(("row", "col"), None), P(), P())
    return jax.shard_map(
        body, mesh=mesh, in_specs=placed, out_specs=P("row", "col"), check_vma=False
    )
```

```python
import jax
import jax.numpy as jnp
from jax import lax
from jax.experimental import pallas as pl
from jax.experimental.pallas import tpu as pltpu
from jax.sharding import PartitionSpec as P

BLOCK = 128
NX, NY, NZL, NZH, NC = 4, 8, 4, 3, 2
NT = 3
F32, BF16 = jnp.float32, jnp.bfloat16
MESH = pl.DeviceIdType.MESH

GATHER = [(0, 0, 256), (0, 256, 256), (1, 0, 256), (1, 256, 256), (2, 0, 256), (2, 256, 256)]
REDUCE = [(0, 0, 1, False, False), (0, 1, 1, False, False), (1, 0, 1, False, False), (1, 1, 1, False, False), (2, 0, 1, True, True), (2, 1, 1, True, True)]

SITES = {}
TOTAL = 0


def site(name, count=1):
    global TOTAL
    SITES[name] = TOTAL
    TOTAL += count


for a in range(len(GATHER)):
    site(("z", a), 4)
    for hop in range(1, 5):
        for side in "RL":
            site(("y", a, hop, side), 2)
for u in range(len(REDUCE)):
    site(("cx", u))
    site(("x", u), 6)
    site(("qc", u))
    site(("q", u), 8)
site("f", 12)
site("gz", 3)
for side in "RL":
    site(("gx", side), 2)


def kernel(a_hbm, g_hbm, ap_hbm, gp_hbm, out_ref, a_buf, g_buf, ap_buf, gp_buf, at, gm, gs, gr, grt, po, pm, cx, xr,
           q, qcr, yr, zr, fin, load_sem, ssem, rsem):
    row, col = lax.axis_index("row"), lax.axis_index("col")
    y, zl = row // NZL, row % NZL
    x, zh, core = col // (NZH * NC), (col // NC) % NZH, col % NC
    sib = 1 - core

    places = {"x": (x, NX), "y": (y, NY), "zl": (zl, NZL), "zh": (zh, NZH)}
    known = {}

    def near(axis, d):
        here, n = places[axis]
        if d % n == 0:
            return here
        if (axis, d % n) not in known:
            known[axis, d % n] = lax.rem(here + d % n, n)
        return known[axis, d % n]

    def at_device(xx, yy, zz, hh, cc):
        return (yy * NZL + zz, xx * (NZH * NC) + hh * NC + cc)

    def dev(dx=0, dy=0, dzl=0, dzh=0, other=False):
        key = (dx % NX, dy % NY, dzl % NZL, dzh % NZH, other)
        if key not in known:
            known[key] = at_device(near("x", dx), near("y", dy), near("zl", dzl), near("zh", dzh), sib if other else core)
        return known[key]

    loads = [pltpu.make_async_copy(src, dst, load_sem.at[i]) for i, (src, dst) in enumerate(
        [(g_hbm, g_buf), (gp_hbm, gp_buf), (ap_hbm, ap_buf), (a_hbm, a_buf)])]
    for load in loads:
        load.start()

    barrier = pltpu.get_barrier_semaphore()
    peers = [dev(dzh=h) for h in range(1, NZH)] + [dev(dzl=i, other=o) for i in range(NZL) for o in (False, True) if i or o]
    peers += [dev(dy=1), dev(dy=-1)] + [dev(dx=d) for d in range(1, NX)]
    for peer in peers:
        pl.semaphore_signal(barrier, inc=1, device_id=peer, device_id_type=MESH)

    drains = []

    def copy_of(name, k, src, dst, to, rk=None):
        i = SITES[name] + k
        return pltpu.make_async_remote_copy(
            src_ref=src, dst_ref=dst, send_sem=ssem.at[i], recv_sem=rsem.at[i if rk is None else SITES[name] + rk],
            device_id=to, device_id_type=MESH)

    def send(name, k, src, dst, to, rk=None):
        copy = copy_of(name, k, src, dst, to, rk)
        copy.start()
        drains.append(copy)

    def arrived(name, k, dst):
        copy_of(name, k, dst, dst, dev(dy=1)).wait_recv()

    def drain():
        while drains:
            drains.pop(0).wait_send()

    loads[0].wait()
    loads[1].wait()
    own_block = row * 6 + col // 4
    lanes = lax.broadcasted_iota(jnp.int32, (12, 192), 1)
    keep = jnp.sum(jnp.where(lanes == own_block, gp_buf[...].astype(F32), 0.0), axis=1, keepdims=True)
    for p in range(12):
        part = slice(p * BLOCK, (p + 1) * BLOCK)
        gm[:, part] = (g_buf[:, part].astype(F32) * jnp.broadcast_to(keep[p:p + 1, :], (32, BLOCK))).astype(BF16)
    me_m = x * NZH + zh

    def lay_out(t):
        jj = near("zh", 1 + t)
        blocks = [gm[:, pl.ds(pl.multiple_of(xx * 384 + jj * BLOCK, BLOCK), BLOCK)] for xx in range(NX)]
        gs[t, y, zl] = jnp.concatenate([b[:, h * 64:(h + 1) * 64] for h in range(2) for b in blocks], axis=1)

    lay_out(0)

    pl.semaphore_wait(barrier, len(peers))

    def z_slab(a, zz):
        t, lane, width = GATHER[a]
        return gs.at[t, y, zz, :, pl.ds(lane, width)]

    own_pair = pl.multiple_of(zl // 2 * 2, 2)
    far_pair = pl.multiple_of(2 - own_pair, 2)
    near_step = 3 - 2 * (zl % 2)

    def pair(a, yy, p):
        t, lane, width = GATHER[a]
        return gs.at[t, near("y", yy), pl.ds(far_pair if p else own_pair, 2), :, pl.ds(lane, width)]

    def z0(a):
        for i in (1, 3, 2):
            send(("z", a), i, z_slab(a, zl), z_slab(a, zl), dev(dzl=i))

    def out_y(a, hop, p, right=True, left=True):
        if right and (hop < 4 or p == 0):
            ref = pair(a, 1 - hop, p)
            send(("y", a, hop, "R"), p, ref, ref, dev(dy=1))
        if left and (hop < 4 or p == 1):
            ref = pair(a, hop - 1, p)
            send(("y", a, hop, "L"), p, ref, ref, dev(dy=-1))

    def o1(a, p):
        if p == 0:
            arrived(("z", a), near_step, z_slab(a, zl + 1 - 2 * (zl % 2)))
        else:
            arrived(("z", a), 2, z_slab(a, near("zl", 2)))
            arrived(("z", a), 4 - near_step, z_slab(a, 3 - zl))
        out_y(a, 1, p)

    def fw(a, hop, side, p):
        arrived(("y", a, hop - 1, side), p, pair(a, 1 - hop if side == "R" else hop - 1, p))
        out_y(a, hop, p, right=side == "R", left=side == "L")

    def h5(a):
        arrived(("y", a, 3, "L"), 0, pair(a, 3, 0))
        arrived(("y", a, 3, "R"), 1, pair(a, -3, 1))
        arrived(("y", a, 4, "R"), 0, pair(a, -4, 0))
        arrived(("y", a, 4, "L"), 1, pair(a, 4, 1))

    def prepare_a():
        loads[2].wait()
        loads[3].wait()
        ap = ap_buf[...].astype(F32).astype(BF16)
        want = lax.broadcasted_iota(jnp.int32, (8, 192), 0) + row * 6
        pick = jnp.where(want == lax.broadcasted_iota(jnp.int32, (8, 192), 1), 1.0, 0.0).astype(BF16)
        rows = jnp.dot(pick, ap, preferred_element_type=F32).astype(BF16)
        want = (lax.broadcasted_iota(jnp.int32, (192, 1024), 1) // 32) * 6 + col // 4
        pick = jnp.where(want == lax.broadcasted_iota(jnp.int32, (192, 1024), 0), 1.0, 0.0).astype(BF16)
        mask = jnp.dot(rows, pick, preferred_element_type=F32)
        for b in range(6):
            block = a_buf[:, :, b * BLOCK:(b + 1) * BLOCK].reshape(1024, BLOCK)
            turned = (block.T.astype(F32) * mask[b:b + 1, :]).astype(BF16)
            for i in range(4):
                at[i % 2, (2 * b + i // 2) * 32:(2 * b + i // 2 + 1) * 32, :] = turned[i * 32:(i + 1) * 32]

    def g0():
        own = gr.at[pl.ds(pl.multiple_of(me_m * 32, 32), 32)]
        for h in range(1, NZH):
            send("gz", h, own, own, dev(dzh=h))

    def gx_rows(dx, first=0, count=96):
        return gr.at[pl.ds(pl.multiple_of(near("x", dx) * 96 + first, 16), count)]

    def g1():
        for h in range(1, NZH):
            m = x * NZH + near("zh", -h)
            arrived("gz", h, gr.at[pl.ds(pl.multiple_of(m * 32, 32), 32)])
        send(("gx", "R"), 0, gx_rows(0), gx_rows(0), dev(dx=1))
        send(("gx", "L"), 0, gx_rows(0), gx_rows(0), dev(dx=-1))

    def g2():
        arrived(("gx", "R"), 0, gx_rows(-1))
        send(("gx", "R"), 1, gx_rows(-1, 0, 48), gx_rows(-1, 0, 48), dev(dx=1))
        arrived(("gx", "L"), 0, gx_rows(1))
        send(("gx", "L"), 1, gx_rows(1, 48, 48), gx_rows(1, 48, 48), dev(dx=-1))

    def g3():
        arrived(("gx", "R"), 1, gx_rows(-2, 0, 48))
        arrived(("gx", "L"), 1, gx_rows(2, 48, 48))
        for b in range(3):
            part = slice(b * BLOCK, (b + 1) * BLOCK)
            grt[:, part] = gr[part, :].T

    def halves(u):
        return REDUCE[u][0], range(REDUCE[u][1], REDUCE[u][1] + REDUCE[u][2]), pl.ds(REDUCE[u][1], REDUCE[u][2])

    def s0(u):
        t, hs, ds = halves(u)
        for half, out in ((sib, po), (core, pm)):
            for h in hs:
                b = gs[t, :, :, :, h * 256:(h + 1) * 256].reshape(1024, 256)
                r = jnp.dot(at[half], b, preferred_element_type=F32)
                for xx in range(NX):
                    part = r[:, xx * 64:(xx + 1) * 64]
                    out[t, h, xx] = jnp.concatenate([part[:192], part[192:]], axis=1)
            if out is po:
                send(("cx", u), 0, po.at[t, ds], cx.at[t, ds], dev(other=True))

    xp, xm, xo = near("x", 1), near("x", -1), near("x", 2)
    A, B, ALL = pl.ds(0, 96), pl.ds(96, 96), pl.ds(0, 192)

    def s1(u):
        t, hs, ds = halves(u)
        arrived(("cx", u), 0, cx.at[t, ds])
        name = ("x", u)

        def add(xx):
            for h in hs:
                pm[t, h, xx] += cx[t, h, xx]

        add(xo)
        if REDUCE[u][3]:
            send(name, 0, pm.at[t, ds, xo], xr.at[t, ds, 0], dev(dx=2))
            add(xp)
            send(name, 1, pm.at[t, ds, xp], xr.at[t, ds, 1], dev(dx=1))
            add(xm)
            send(name, 2, pm.at[t, ds, xm], xr.at[t, ds, 2], dev(dx=-1))
        else:
            send(name, 0, pm.at[t, ds, xo, A], xr.at[t, ds, 0, A], dev(dx=1))
            send(name, 3, pm.at[t, ds, xo, B], xr.at[t, ds, 0, B], dev(dx=-1))
            add(xp)
            send(name, 1, pm.at[t, ds, xp, B], xr.at[t, ds, 1, B], dev(dx=1))
            add(xm)
            send(name, 4, pm.at[t, ds, xm, A], xr.at[t, ds, 2, A], dev(dx=-1))
        add(x)

    def s2(u):
        t, hs, ds = halves(u)
        name = ("x", u)
        arrived(name, 0, xr.at[t, ds, 0, A])
        for h in hs:
            pm[t, h, xp, A] += xr[t, h, 0, A]
        send(name, 2, pm.at[t, ds, xp, A], xr.at[t, ds, 1, A], dev(dx=1))
        arrived(name, 3, xr.at[t, ds, 0, B])
        for h in hs:
            pm[t, h, xm, B] += xr[t, h, 0, B]
        send(name, 5, pm.at[t, ds, xm, B], xr.at[t, ds, 2, B], dev(dx=-1))

    def s3(u):
        t, hs, ds = halves(u)
        name = ("x", u)
        if REDUCE[u][3]:
            for k in range(3):
                arrived(name, k, xr.at[t, ds, k])
        else:
            arrived(name, 1, xr.at[t, ds, 1, B])
            arrived(name, 4, xr.at[t, ds, 2, A])
            arrived(name, 2, xr.at[t, ds, 1, A])
            arrived(name, 5, xr.at[t, ds, 2, B])
        pieces = []
        for h in hs:
            total = pm[t, h, x] + (xr[t, h, 1] + xr[t, h, 2])
            if REDUCE[u][3]:
                total = total + xr[t, h, 0]
            total = jnp.concatenate([total[:, :64], total[:, 64:]], axis=0)
            high = total.astype(BF16)
            pieces += [high, (total - high.astype(F32)).astype(BF16)]
        r = jnp.dot(grt[...], jnp.concatenate(pieces, axis=1), preferred_element_type=F32)
        for n, h in enumerate(hs):
            v = (r[:, n * BLOCK:n * BLOCK + 64] + r[:, n * BLOCK + 64:(n + 1) * BLOCK]).reshape(32, 2, 24, 64)
            v = jnp.concatenate([v[:, 0], v[:, 1]], axis=2).reshape(NY, NC, 2, 24, BLOCK)
            for k in range(NC):
                q[t, h, k] = v[:, k]
        send(("qc", u), 0, q.at[t, ds, sib], qcr.at[t, ds], dev(other=True))

    def q_to(u, dy, p=None):
        t, hs, ds = halves(u)
        return q.at[t, ds, core, near("y", dy), pl.ds(0, 2) if p is None else pl.ds(p, 1)]

    def y_slot(u, k, p=None):
        t, hs, ds = halves(u)
        return yr.at[t, ds, k, pl.ds(0, 2) if p is None else pl.ds(p, 1)]

    def s4(u):
        t, hs, ds = halves(u)
        arrived(("qc", u), 0, qcr.at[t, ds])
        for h in hs:
            q[t, h, core] += qcr[t, h]
        if REDUCE[u][4]:
            for d in (4, 3, 5, 2, 6, 1, 7):
                send(("q", u), d, q_to(u, d), y_slot(u, d), dev(dy=d))
        else:
            send(("q", u), 0, q_to(u, 4, 0), y_slot(u, 0, 0), dev(dy=1))
            send(("q", u), 4, q_to(u, -4, 1), y_slot(u, 4, 1), dev(dy=-1))

    def y_step(u, k):
        if REDUCE[u][4]:
            return
        for side, sign in ((0, 1), (1, -1)):
            p = side if k == 1 else None
            slot = y_slot(u, 4 * side + k - 1, p)
            arrived(("q", u), 4 * side + k - 1, slot)
            own = q_to(u, sign * (4 - k), p)
            own[...] += slot[...]
            send(("q", u), 4 * side + k, q_to(u, sign * (4 - k)), y_slot(u, 4 * side + k), dev(dy=sign))

    def s5(u):
        y_step(u, 1)

    def s6(u):
        y_step(u, 2)

    def s7(u):
        y_step(u, 3)

    def s8(u):
        t, hs, ds = halves(u)
        slots = range(1, 8) if REDUCE[u][4] else (3, 7)
        for k in slots:
            arrived(("q", u), k, y_slot(u, k))
        for h in hs:
            total = q[t, h, core, y]
            for k in slots:
                total = total + yr[t, h, k]
            fin[t, h] = total
            for b in range(2):
                last = f_copy(t, h, b)
                if t < 2:
                    last.start()
                else:
                    mine = f_mine(h, b)
                    pl.when(jnp.logical_not(mine))(last.start)

                    @pl.when(mine)
                    def _():
                        zr[2, 0] = fin[2, h, b]

    def f_mine(h, b):
        return jnp.logical_and(zl == 2 * core + b, core == h)

    def f_copy(t, h, b):
        zz = 2 * core + b
        i = lax.rem(zz - zl + NZL, NZL)
        return copy_of("f", t * 4 + h * 2 + b, fin.at[t, h, b], zr.at[t, i],
                       at_device(x, y, zz, near("zh", t + 1), h), rk=t * 4 + i)

    def finish():
        for t in range(NT):
            for i in range(NZL):
                def wait(t=t, i=i):
                    arrived("f", t * 4 + i, zr.at[t, i])
                if t < 2 or i:
                    wait()
                else:
                    pl.when(core != zl // 2)(wait)
        total = zr[0, 0]
        for n in range(1, 12):
            total = total + zr[n // 4, n % 4]
        out_ref[0:24, :] = total[:, :64]
        out_ref[24:48, :] = total[:, 64:]
        for t in range(NT):
            for h in range(NC):
                for b in range(2):
                    last = f_copy(t, h, b)
                    if t < 2:
                        last.wait_send()
                    else:
                        pl.when(jnp.logical_not(f_mine(h, b)))(last.wait_send)

    z0(0)
    lay_out(1)
    lay_out(2)
    gr[pl.ds(pl.multiple_of(me_m * 32, 32), 32), :] = gm[...]
    z0(1)
    z0(2)
    g0()
    z0(3)
    z0(4)
    z0(5)
    prepare_a()
    o1(0,0)
    o1(0,1)
    o1(1,0)
    o1(1,1)
    fw(0,2,"R",0)
    fw(0,2,"L",0)
    fw(0,2,"R",1)
    fw(0,2,"L",1)
    fw(1,2,"R",0)
    fw(1,2,"L",0)
    fw(1,2,"R",1)
    fw(1,2,"L",1)
    o1(2,0)
    o1(2,1)
    fw(0,3,"R",0)
    fw(0,3,"L",0)
    fw(0,3,"R",1)
    fw(0,3,"L",1)
    fw(1,3,"R",0)
    fw(1,3,"L",0)
    fw(1,3,"R",1)
    fw(1,3,"L",1)
    fw(2,2,"R",0)
    fw(2,2,"L",0)
    fw(2,2,"R",1)
    fw(2,2,"L",1)
    o1(3,0)
    fw(0,4,"R",0)
    fw(0,4,"L",1)
    g1()
    fw(1,4,"R",0)
    o1(3,1)
    o1(5,0)
    fw(1,4,"L",1)
    fw(2,3,"R",0)
    fw(2,3,"L",0)
    fw(2,3,"R",1)
    fw(2,3,"L",1)
    o1(5,1)
    fw(3,2,"R",0)
    fw(3,2,"L",0)
    h5(0)
    s0(0)
    fw(3,2,"L",1)
    fw(3,2,"R",1)
    fw(5,2,"L",0)
    fw(5,2,"R",0)
    h5(1)
    s0(1)
    fw(2,4,"R",0)
    s1(0)
    fw(2,4,"L",1)
    fw(5,2,"R",1)
    fw(5,2,"L",1)
    s1(1)
    fw(3,3,"L",0)
    g2()
    fw(3,3,"R",0)
    fw(3,3,"R",1)
    fw(3,3,"L",1)
    o1(4,0)
    o1(4,1)
    fw(5,3,"R",0)
    fw(5,3,"L",0)
    s2(0)
    h5(2)
    s0(2)
    fw(5,3,"R",1)
    fw(5,3,"L",1)
    fw(3,4,"R",0)
    s2(1)
    fw(3,4,"L",1)
    s1(2)
    fw(4,2,"L",0)
    fw(4,2,"R",0)
    fw(4,2,"R",1)
    fw(4,2,"L",1)
    fw(5,4,"R",0)
    fw(5,4,"L",1)
    h5(3)
    s0(3)
    g3()
    fw(4,3,"L",0)
    fw(4,3,"R",0)
    fw(4,3,"R",1)
    s3(0)
    fw(4,3,"L",1)
    s1(3)
    s3(1)
    s4(0)
    s2(2)
    h5(5)
    s0(5)
    fw(4,4,"R",0)
    s4(1)
    fw(4,4,"L",1)
    s2(3)
    s1(5)
    s5(0)
    s5(1)
    s3(2)
    h5(4)
    s0(4)
    s3(3)
    s6(0)
    s4(2)
    s6(1)
    s1(4)
    s4(3)
    s7(0)
    s5(2)
    s3(5)
    s7(1)
    s5(3)
    s4(5)
    s8(0)
    s6(2)
    s8(1)
    s3(4)
    s6(3)
    s4(4)
    s8(5)
    s7(2)
    s7(3)
    s8(4)
    s8(2)
    s8(3)
    finish()
    drain()


def body(curl_tiles, gradient, a_pattern, g_pattern):
    hbm = pl.BlockSpec(memory_space=pl.ANY)
    return pl.pallas_call(
        kernel,
        out_shape=jax.ShapeDtypeStruct((48, 64), F32),
        in_specs=[hbm] * 4,
        out_specs=pl.BlockSpec(memory_space=pltpu.VMEM),
        scratch_shapes=[
            pltpu.VMEM((32, 32, 768), BF16),
            pltpu.VMEM((32, 1536), BF16),
            pltpu.VMEM((192, 192), jnp.int32),
            pltpu.VMEM((12, 192), jnp.int32),
            pltpu.VMEM((2, 384, 1024), BF16),
            pltpu.VMEM((32, 1536), BF16),
            pltpu.VMEM((NT, NY, NZL, 32, 512), BF16),
            pltpu.VMEM((384, 1536), BF16),
            pltpu.VMEM((1536, 384), BF16),
            pltpu.VMEM((NT, 2, NX, 192, BLOCK), F32),
            pltpu.VMEM((NT, 2, NX, 192, BLOCK), F32),
            pltpu.VMEM((NT, 2, NX, 192, BLOCK), F32),
            pltpu.VMEM((NT, 2, 3, 192, BLOCK), F32),
            pltpu.VMEM((NT, 2, NC, NY, 2, 24, BLOCK), F32),
            pltpu.VMEM((NT, 2, NY, 2, 24, BLOCK), F32),
            pltpu.VMEM((NT, 2, 8, 2, 24, BLOCK), F32),
            pltpu.VMEM((NT, NZL, 24, BLOCK), F32),
            pltpu.VMEM((NT, 2, 2, 24, BLOCK), F32),
            pltpu.SemaphoreType.DMA((4,)),
            pltpu.SemaphoreType.DMA((TOTAL,)),
            pltpu.SemaphoreType.DMA((TOTAL,)),
        ],
        compiler_params=pltpu.CompilerParams(
            collective_id=0, has_side_effects=True, vmem_limit_bytes=60 * 1024 * 1024),
    )(curl_tiles, gradient, a_pattern, g_pattern.T)


def solution(mesh):
    placed = (P(None, "col", "row"), P(("row", "col"), None), P(), P())
    return jax.shard_map(
        body, mesh=mesh, in_specs=placed, out_specs=P("row", "col"), check_vma=False
    )
```
